768 devices in a mesh: rep: 96 (over y_hi, z, x), tp: 8 (over y_lo, core).
Axes of the slice: x: 4, y: 8 (y_hi: 2, y_lo: 4; y = y_hi * 4 + y_lo), z: 12, core: 2. Of those that a mesh axis runs over, the one named last changes fastest.
Arguments:
- loader_rows: bfloat16 [24576, 1792], P('rep', 'tp'), may hold values from -14 to 14
- pack_dest: int32 [24576], P('rep'), may hold values from 0 to 24575, as said below
- segment_ids: int32 [96, 256], P('rep'), may hold values from 0 to 11, never falling along the last dimension, each value on 1 to 64 neighbouring positions
- w_qkv: bfloat16 [1792, 3, 1792], P(None, None, 'tp'), may hold values from -0.125 to 0.125
- w_out: bfloat16 [1792, 1792], P('tp'), may hold values from -0.125 to 0.125
- d_out: bfloat16 [24576, 1792], P('rep', 'tp'), may hold values from -6 to 6
Outputs:
- grad_qkv: float32 [5376, 1792], P('rep', 'tp')
- d_packed: bfloat16 [24576, 1792], P('rep', 'tp')
The draws below stay inside these ranges and needn't reach their ends.
Inputs may be any that keep to these rules, and one draw needn't show every extreme that they name: `pack_dest`: a permutation of all rows; every pack receives at most 3 rows from one loader shard, and exactly 3 from some.
All inputs are finite; a program needn't handle non-finite values.
Results may differ from the reference program's by a relative error of at most 0.034.
The reference program's roundings to bfloat16 on the way (of `packed`, `qkv`, `probs_b`, `attn`, `d_attn`, `d_score` and `d_qkv`) count: a program that leaves them out, or rounds other values in their place, can miss the bound.
Values may be sent and summed in bfloat16 or wider, within the bound.
A program may use at most 64 MiB of HBM per device.

```python
import math
import jax
import jax.numpy as jnp
import numpy as np
from jax import lax

D = 1792
HEADS = 16
HEAD_DIM = 112
TOK_DEV = 256
IMAGES = 12
PACKS = 96
TOKENS = 24576
IMAGE_MOST = 64


def draw_loader_rows(key, part):
    key = jax.random.fold_in(key, 5)
    first = jax.random.fold_in(key, 0)
    rows = jnp.clip(jax.random.normal(first, (TOKENS, D), jnp.float32), -6.0, 6.0)
    return rows.astype(jnp.bfloat16)


def draw_pack_dest(key, part):
    key = jax.random.fold_in(key, 11)
    first, second, third, fourth = jax.random.split(key, 4)
    count = PACKS
    per_pack = TOK_DEV
    whole = per_pack // count
    extra = per_pack % count
    sigma = jax.random.permutation(first, count)
    tau_perm = jax.random.permutation(second, count)
    counts = whole + ((sigma[None, :] - tau_perm[:, None]) % count < extra).astype(jnp.int32)
    offsets = jnp.cumsum(counts, axis=0) - counts
    starts = jnp.cumsum(counts, axis=1) - counts
    slot_perms = jax.vmap(lambda one: jax.random.permutation(one, per_pack))(jax.random.split(third, count))
    row_perms = jax.vmap(lambda one: jax.random.permutation(one, per_pack))(jax.random.split(fourth, count))

    def one_source(source):
        dest_list = jnp.repeat(jnp.arange(count, dtype=jnp.int32), counts[source], total_repeat_length=per_pack)
        within = jnp.arange(per_pack, dtype=jnp.int32) - starts[source, dest_list]
        slot_first = offsets[source, dest_list] + within
        slot_final = slot_perms[dest_list, slot_first]
        glob = dest_list * per_pack + slot_final
        return glob[row_perms[source]]
    table = jax.vmap(one_source)(jnp.arange(count, dtype=jnp.int32))
    return table.reshape(count * per_pack).astype(jnp.int32)


def steps_of(key, dims, pieces, low, largest):
    level = 1.0
    for position, parts in pieces:
        heights = jax.random.uniform(jax.random.fold_in(jax.random.fold_in(key, 6), position), (parts,), jnp.float32, low / len(pieces), largest / len(pieces))
        level = level * jnp.repeat(jnp.exp(heights), dims[position] // parts).reshape((-1,) + (1,) * (len(dims) - 1 - position))
    return level


def length_profile(number_of, total, limit, lean):
    portions = [(1 << 20) // math.isqrt(rank ** lean) + 1 for rank in range(2, number_of + 1)]
    spare, given = total - limit - (number_of - 1), [1] * (number_of - 1)
    while spare > 0:
        candidates = [i for i in range(number_of - 1) if given[i] < limit]
        mass, remaining = sum([portions[i] for i in candidates]), spare
        for i in candidates:
            more = min(limit - given[i], max(1, remaining * portions[i] // mass), spare)
            given[i] = given[i] + more
            spare = spare - more
    return np.array([limit] + given)


def uneven(rng, amount, total, reach, skew):
    if amount == 2:
        one = jax.random.randint(rng, (), max(1, total - reach), min(reach, total - 1) + 1)
        return jnp.stack([one, total - one])
    tallies = jnp.asarray(length_profile(amount, total, reach, skew), jnp.int32)
    couples = (amount - 1) // 2
    giver, taker = tallies[1:1 + 2 * couples:2], tallies[2:2 + 2 * couples:2]
    room = jnp.minimum(giver - 1, reach - taker)
    passed = jax.random.randint(jax.random.fold_in(rng, 1), (couples,), 0, 1 << 20) % (room + 1)
    tallies = tallies.at[1:1 + 2 * couples:2].set(giver - passed).at[2:2 + 2 * couples:2].set(taker + passed)
    return tallies[jax.random.permutation(jax.random.fold_in(rng, 2), amount)]


def normal_values(own_key, dims, scale, reach, pieces=(), kind=jnp.bfloat16):
    level = steps_of(own_key, dims, pieces, -0.22, 0.18) if pieces else 1.0
    entries = jax.random.normal(own_key, dims, jnp.float32) * scale * level
    return jnp.minimum(jnp.maximum(entries, -reach), reach).astype(kind)


def setup_inputs(seed: int = 0) -> dict:
    arg_keys = jax.random.split(jax.random.key(seed), 7)
    return {
        "loader_rows": draw_loader_rows(jax.random.fold_in(arg_keys[6], 71), 0),
        "pack_dest": draw_pack_dest(jax.random.fold_in(arg_keys[6], 71), 0),
        "segment_ids": jax.vmap(lambda own: jnp.searchsorted(jnp.cumsum(uneven(own, IMAGES, TOK_DEV, IMAGE_MOST, 2)), jnp.arange(TOK_DEV), side="right"))(jax.random.split(arg_keys[2], PACKS)).reshape((PACKS, TOK_DEV)).astype(jnp.int32),
        "w_qkv": normal_values(arg_keys[3], (D, 3, HEADS * HEAD_DIM), D ** -0.5, 0.125, ((2, 8),)),
        "w_out": normal_values(arg_keys[4], (HEADS * HEAD_DIM, D), (HEADS * HEAD_DIM) ** -0.5, 0.125, ((0, 8),)),
        "d_out": normal_values(arg_keys[5], (TOKENS, D), 1.0, 6.0, ((0, 96), (1, 8))),
    }


def reference(loader_rows, pack_dest, segment_ids, w_qkv, w_out, d_out):
    scale = HEAD_DIM ** -0.5
    packed = jnp.zeros((TOKENS, D), jnp.bfloat16).at[pack_dest].set(loader_rows)
    rows_all = packed.reshape(PACKS, TOK_DEV, D)
    cot_all = d_out.reshape(PACKS, TOK_DEV, D)
    weights = w_qkv.astype(jnp.float32)

    def one_pack(carry, inputs):
        rows, seg, cot = inputs
        qkv = jnp.einsum('td,dwc->twc', rows.astype(jnp.float32), weights).astype(jnp.bfloat16)
        qkv = qkv.reshape(TOK_DEV, 3, HEADS, HEAD_DIM).astype(jnp.float32)
        query, keys, values = qkv[:, 0], qkv[:, 1], qkv[:, 2]
        scores = jnp.einsum('qhe,khe->hqk', query, keys) * scale
        same = seg[:, None] == seg[None, :]
        scores = jnp.where(same[None], scores, -jnp.inf)
        expo = jnp.exp(scores - jnp.max(scores, axis=2, keepdims=True))
        probs = expo / jnp.sum(expo, axis=2, keepdims=True)
        probs_b = probs.astype(jnp.bfloat16).astype(jnp.float32)
        attn = jnp.einsum('hqk,khe->qhe', probs_b, values).astype(jnp.bfloat16).astype(jnp.float32)
        d_attn = jnp.dot(cot, w_out.T, preferred_element_type=jnp.float32).astype(jnp.bfloat16)
        d_attn = d_attn.reshape(TOK_DEV, HEADS, HEAD_DIM).astype(jnp.float32)
        d_prob = jnp.einsum('qhe,khe->hqk', d_attn, values)
        delta = jnp.einsum('qhe,qhe->hq', d_attn, attn)
        d_score = (probs * (d_prob - delta[:, :, None]) * scale).astype(jnp.bfloat16).astype(jnp.float32)
        d_query = jnp.einsum('hqk,khe->qhe', d_score, keys).astype(jnp.bfloat16)
        d_keys = jnp.einsum('hqk,qhe->khe', d_score, query).astype(jnp.bfloat16)
        d_values = jnp.einsum('hqk,qhe->khe', probs_b, d_attn).astype(jnp.bfloat16)
        d_qkv = jnp.stack([d_query, d_keys, d_values], axis=1).reshape(TOK_DEV, 3, HEADS * HEAD_DIM)
        d_qkv = d_qkv.astype(jnp.float32)
        carry = carry + jnp.einsum('td,twc->dwc', rows.astype(jnp.float32), d_qkv)
        d_rows = jnp.einsum('twc,dwc->td', d_qkv, weights).astype(jnp.bfloat16)
        return carry, d_rows

    start = jnp.zeros((D, 3, HEADS * HEAD_DIM), jnp.float32)
    total, d_rows = lax.scan(one_pack, start, (rows_all, segment_ids, cot_all))
    grad_qkv = total.reshape(3 * D, HEADS * HEAD_DIM) * (TOKENS ** -0.5)
    return grad_qkv, d_rows.reshape(TOKENS, D)
```

```python
import functools

import jax
import jax.numpy as jnp
import numpy as np
from jax import lax
from jax.experimental import pallas as pl
from jax.experimental.pallas import tpu as pltpu
from jax.sharding import PartitionSpec as P

HEAD_DIM = 112
MESH = pl.DeviceIdType.MESH
F32 = jnp.float32
BF16 = jnp.bfloat16


def _dot(a, b, ca, cb):
    return lax.dot_general(a, b, (((ca,), (cb,)), ((), ())), preferred_element_type=F32)


def _nn(a, b):
    return _dot(a, b, 1, 0)


def _nt(a, b):
    return _dot(a, b, 1, 1)


def _tn(a, b):
    return _dot(a, b, 0, 0)


def _onehot(cond):
    return jnp.where(cond, 1.0, 0.0).astype(BF16)


class Sizes:
    def __init__(self, yh, z, x, yl, c, tok, width):
        self.YH, self.Z, self.X, self.YL, self.C = yh, z, x, yl, c
        self.TOK, self.W = tok, width
        self.R, self.T = yh * z * x, yl * c
        self.D = width * self.T
        self.Q = yh * x
        self.CAP = -(-tok // self.R)
        self.B1 = -(-self.Q * self.CAP // 16) * 16
        self.B2 = -(-self.Z * self.CAP // 16) * 16
        self.RPD = 3 * self.D // self.R
        self.RZ = x * self.RPD


def _regroup(s):
    m = np.zeros((s.Q * s.B2, s.Z * s.B1), np.float32)
    for q in range(s.Q):
        for zs in range(s.Z):
            for j in range(s.CAP):
                m[q * s.B2 + zs * s.CAP + j, zs * s.B1 + q * s.CAP + j] = 1.0
    return m


def _kernel(
    s,
    ld, dest, seg, w_hbm, wo_hbm, cot, regroup,
    g_out, d_out,
    wv, wn, wo, s1, r1, s2, r2, xt, ct, dq3, f0, f1, stage, slots, red, xs, xr, acc, yr,
    ps_s, ps_r, pown, py_s, py_r,
    w_sem, z_ss, z_rs, q_ss, q_rs, cg_ss, cg_rs, cf_ss, cf_rs, xg_ss, xg_rs, xf_ss, xf_rs,
    c_ss, c_rs, x_ss, x_rs, y_ss, y_rs, pc_ss, pc_rs, py_ss, py_rs,
):
    W, TOK, Z, X, YH, YL, C, Q = s.W, s.TOK, s.Z, s.X, s.YH, s.YL, s.C, s.Q
    rep, tp = lax.axis_index("rep"), lax.axis_index("tp")
    mx = rep % X
    mz = (rep // X) % Z
    my = rep // (X * Z)
    ml, mc = tp // C, tp % C
    mq = my * X + mx

    def at_z(z):
        return {"rep": (my * Z + z) * X + mx}

    def at_q(q):
        return {"rep": ((q // X) * Z + mz) * X + q % X}

    def at_t(l, c):
        return {"tp": l * C + c}

    def rows(ref, start, size, unit):
        return ref.at[pl.ds(pl.multiple_of(start, unit), size)]

    def send(src, dst, ss, rs, device):
        copy = pltpu.make_async_remote_copy(
            src_ref=src, dst_ref=dst, send_sem=ss, recv_sem=rs, device_id=device, device_id_type=MESH
        )
        copy.start()
        return copy

    partners = [at_z((mz + o) % Z) for o in range(1, Z)]
    partners += [at_q((mq + o) % Q) for o in range(1, Q)]
    partners += [at_t((ml + o) % YL, mc) for o in range(1, YL)]
    partners += [at_t(ml, 1 - mc)]
    barrier = pltpu.get_barrier_semaphore()
    for device in partners:
        pl.semaphore_signal(barrier, inc=1, device_id=device, device_id_type=MESH)

    w_copy = pltpu.make_async_copy(w_hbm, wv, w_sem.at[0])
    w_copy.start()
    wo_copy = pltpu.make_async_copy(wo_hbm, wo, w_sem.at[1])
    wo_copy.start()

    dst = dest[...]
    pack, slot = dst // TOK, dst % TOK
    iota_p = lax.broadcasted_iota(jnp.int32, (128, TOK), 0)
    of_pack = _onehot(iota_p == pack)
    before = _onehot(
        lax.broadcasted_iota(jnp.int32, (TOK, TOK), 0) < lax.broadcasted_iota(jnp.int32, (TOK, TOK), 1)
    )
    rank = jnp.sum(_nn(of_pack, before) * of_pack.astype(F32), axis=0, keepdims=True).astype(jnp.int32)
    px, pz, py = pack % X, (pack // X) % Z, pack // (X * Z)
    place = pz * s.B1 + (py * X + px) * s.CAP + rank
    pick = _onehot(lax.broadcasted_iota(jnp.int32, (Z * s.B1, TOK), 0) == place)
    slot1 = jnp.broadcast_to((slot + 1).astype(F32), (256 - W, TOK)).astype(BF16)
    s1[...] = _nt(pick, jnp.concatenate([ld[...], slot1], axis=0)).astype(BF16)

    pl.semaphore_wait(barrier, len(partners))

    zc = []
    for o in range(1, Z):
        to = (mz + o) % Z
        zc.append(
            send(rows(s1, to * s.B1, s.B1, 16), rows(r1, mz * s.B1, s.B1, 16),
                 z_ss.at[o - 1], z_rs.at[o - 1], at_z(to))
        )
    r1[pl.ds(pl.multiple_of(mz * s.B1, 16), s.B1)] = s1[pl.ds(pl.multiple_of(mz * s.B1, 16), s.B1)]

    def gather(src, buf, ss, rs, fs, fr):
        mine = rows(buf, tp * W, W, 16)
        first = [send(src, mine, ss.at[o - 1], rs.at[o - 1], at_t((ml + o) % YL, mc)) for o in range(1, YL)]
        first.append(send(src, mine, fs.at[0], fr.at[0], at_t(ml, 1 - mc)))

        def rest():
            more = []
            for o in range(1, YL):
                first[o - 1].wait_recv()
                there = rows(buf, ((ml - o + YL) % YL * C + mc) * W, W, 16)
                more.append(send(there, there, fs.at[o], fr.at[o], at_t(ml, 1 - mc)))
            first[-1].wait_recv()
            for copy in more:
                copy.wait_recv()
            return first + more

        return rest

    cot_rest = gather(cot, ct, cg_ss, cg_rs, cf_ss, cf_rs)
    ct[pl.ds(pl.multiple_of(tp * W, 16), W)] = cot[...]

    w_copy.wait()
    for w in range(3):
        for j in range(0, s.D, 128):
            wn[w, pl.ds(j, 128)] = wv[pl.ds(w * W, W), pl.ds(j, 128)].T

    for copy in zc:
        copy.wait_recv()
    s2[...] = _nn(regroup[...], r1[...]).astype(BF16)
    qc = []
    for o in range(1, Q):
        to = (mq + o) % Q
        qc.append(
            send(rows(s2, to * s.B2, s.B2, 16), rows(r2, mq * s.B2, s.B2, 16),
                 q_ss.at[o - 1], q_rs.at[o - 1], at_q(to))
        )
    r2[pl.ds(pl.multiple_of(mq * s.B2, 16), s.B2)] = s2[pl.ds(pl.multiple_of(mq * s.B2, 16), s.B2)]

    sent = cot_rest()
    wo_copy.wait()
    d_attn = _nn(wo[...], ct[...]).astype(BF16)

    for copy in qc:
        copy.wait_recv()
    got = r2[...]
    slots_got = got[:, W:W + 1].astype(F32)
    iota_s = lax.broadcasted_iota(jnp.int32, (Q * s.B2, TOK), 1).astype(F32) + 1.0
    put = _onehot(slots_got == iota_s)
    xt[pl.ds(pl.multiple_of(tp * W, 16), W)] = _tn(got, put)[:W].astype(BF16)
    rows_rest = gather(rows(xt, tp * W, W, 16), xt, xg_ss, xg_rs, xf_ss, xf_rs)
    sent += rows_rest()

    qkv = _nn(wv[...], xt[...]).astype(BF16)
    scale = HEAD_DIM ** (-0.5)
    seg_to = jnp.broadcast_to(seg[...].astype(F32), (TOK, TOK))
    same = seg_to.T == seg_to
    heads = W // HEAD_DIM
    for h in range(heads):
        lo = h * HEAD_DIM
        qt = qkv[lo:lo + HEAD_DIM]
        kt = qkv[W + lo:W + lo + HEAD_DIM]
        vt = qkv[2 * W + lo:2 * W + lo + HEAD_DIM]
        da = d_attn[lo:lo + HEAD_DIM]
        scores = jnp.where(same, _tn(kt, qt) * scale, -jnp.inf)
        expo = jnp.exp(scores - jnp.max(scores, axis=0, keepdims=True))
        probs = expo / jnp.sum(expo, axis=0, keepdims=True)
        probs_b = probs.astype(BF16)
        attn = _nn(vt, probs_b).astype(BF16)
        d_prob = _tn(vt, da)
        delta = jnp.sum(da.astype(F32) * attn.astype(F32), axis=0, keepdims=True)
        d_score = (probs * (d_prob - delta) * scale).astype(BF16)
        dq3[0, lo:lo + HEAD_DIM] = _nn(kt, d_score).astype(BF16)
        dq3[1, lo:lo + HEAD_DIM] = _nt(qt, d_score).astype(BF16)
        dq3[2, lo:lo + HEAD_DIM] = _nt(da, probs_b).astype(BF16)
    dq3[:, W:] = jnp.zeros((3, 256 - W, TOK), BF16)

    f = (f0, f1)
    for t in range(s.T):
        block = xt[t * W:(t + 1) * W]
        for w in range(3):
            g = _nt(block, dq3[w])
            for h in range(2):
                f[h][pl.ds(t * 3 * W + w, W, stride=3)] = g[:, h * 128:(h + 1) * 128]

    def chunk(h, y, z):
        return f[h][pl.ds(pl.multiple_of((y * Z + z) * s.RZ, 8), s.RZ)]

    steps = Z // 2
    ring = {}

    def ring_step(k):
        for d in range(2):
            sign = 1 if d == 0 else -1
            to = at_z((mz + sign + Z) % Z)
            z = (mz + sign * (steps + 1 - k) + Z) % Z
            for h in range(2):
                if k == 1:
                    stage[d, h] = chunk(h, d, z).astype(BF16)
                    copy = send(stage.at[d, h], slots.at[d, h, 0, pl.ds(d * s.RZ, s.RZ)],
                                c_ss.at[d, h, 0], c_rs.at[d, h, 0], to)
                else:
                    ring[d, h, k - 1].wait_recv()
                    for y in range(YH):
                        part = pl.ds(y * s.RZ, s.RZ)
                        own = chunk(h, y, z)
                        if k > 2 or y == d:
                            own = own + slots[d, h, k - 2, part].astype(F32)
                        slots[d, h, k - 2, part] = own.astype(BF16)
                    copy = send(slots.at[d, h, k - 2], slots.at[d, h, k - 1],
                                c_ss.at[d, h, k - 1], c_rs.at[d, h, k - 1], to)
                ring[d, h, k] = copy

    def part(t):
        t = pl.multiple_of(t * W, 16)
        total = _nn(wn[0, pl.ds(t, W)], dq3[0, :W])
        total += _nn(wn[1, pl.ds(t, W)], dq3[1, :W])
        return total + _nn(wn[2, pl.ds(t, W)], dq3[2, :W])

    ring_step(1)
    for l in range(YL):
        ps_s[l] = part(l * C + 1 - mc).astype(BF16)
    pair = send(ps_s, ps_r, pc_ss, pc_rs, at_t(ml, 1 - mc))
    for l in range(YL):
        pown[l] = part(l * C + mc)
    ring_step(2)
    pair.wait_recv()
    for l in range(YL):
        pown[l] = pown[l] + ps_r[l].astype(F32)
        py_s[l] = pown[l].astype(BF16)
    pc = []
    for o in range(1, YL):
        to = (ml + o) % YL
        pc.append(send(py_s.at[to], py_r.at[o - 1], py_ss.at[o - 1], py_rs.at[o - 1], at_t(to, mc)))
    for k in range(3, steps + 1):
        ring_step(k)
    for copy in pc:
        copy.wait_recv()
    total = pown[ml]
    for o in range(1, YL):
        total = total + py_r[o - 1].astype(F32)
    d_out[...] = total.astype(BF16)

    for h in range(2):
        for y in range(YH):
            part_y = pl.ds(y * s.RZ, s.RZ)
            red[h, part_y] = chunk(h, y, mz)
        for d in range(2):
            ring[d, h, steps].wait_recv()
            for y in range(YH):
                part_y = pl.ds(y * s.RZ, s.RZ)
                red[h, part_y] = red[h, part_y] + slots[d, h, steps - 1, part_y].astype(F32)

    def of_x(h, x):
        return jnp.concatenate(
            [red[h, pl.ds(pl.multiple_of(y * s.RZ + x * s.RPD, 8), s.RPD)] for y in range(YH)], axis=0
        )

    xc = []
    for o in range(1, X):
        to = (mx + o) % X
        for h in range(2):
            xs[o - 1, h] = of_x(h, to).astype(BF16)
        xc.append(send(xs.at[o - 1], xr.at[o - 1], x_ss.at[o - 1], x_rs.at[o - 1], at_q(my * X + to)))
    for h in range(2):
        acc[h] = of_x(h, mx)
    for o in range(1, X):
        xc[o - 1].wait_recv()
        for h in range(2):
            acc[h] = acc[h] + xr[o - 1, h].astype(F32)
    other = 1 - my
    yc = send(acc.at[:, pl.ds(pl.multiple_of(other * s.RPD, 8), s.RPD)], yr, y_ss, y_rs, at_q(other * X + mx))
    yc.wait_recv()
    norm = (TOK * s.R) ** (-0.5)
    mine = pl.ds(pl.multiple_of(my * s.RPD, 8), s.RPD)
    g_out[:, :128] = (acc[0, mine] + yr[0]) * norm
    g_out[:, 128:] = ((acc[1, mine] + yr[1]) * norm)[:, :W - 128]

    for copy in zc + qc + sent + list(ring.values()) + [pair] + pc + xc + [yc]:
        copy.wait_send()


def shards(s, loader_rows, pack_dest, segment_ids, w_qkv, w_out, d_out):
    W, TOK, D = s.W, s.TOK, s.D
    Q, Z, X, YL = s.Q, s.Z, s.X, s.YL
    dma = pltpu.SemaphoreType.DMA
    vmem = pl.BlockSpec(memory_space=pltpu.VMEM)
    hbm = pl.BlockSpec(memory_space=pl.ANY)
    steps = Z // 2
    grad, packed = pl.pallas_call(
        functools.partial(_kernel, s),
        out_shape=(
            jax.ShapeDtypeStruct((s.RPD, W), F32),
            jax.ShapeDtypeStruct((W, TOK), BF16),
        ),
        in_specs=[vmem, vmem, vmem, hbm, hbm, vmem, vmem],
        out_specs=(vmem, vmem),
        scratch_shapes=[
            pltpu.VMEM((3 * W, D), BF16),
            pltpu.VMEM((3, D, W), BF16),
            pltpu.VMEM((W, D), BF16),
            pltpu.VMEM((Z * s.B1, 256), BF16),
            pltpu.VMEM((Z * s.B1, 256), BF16),
            pltpu.VMEM((Q * s.B2, 256), BF16),
            pltpu.VMEM((Q * s.B2, 256), BF16),
            pltpu.VMEM((D, TOK), BF16),
            pltpu.VMEM((D, TOK), BF16),
            pltpu.VMEM((3, 256, TOK), BF16),
            pltpu.VMEM((3 * D, 128), F32),
            pltpu.VMEM((3 * D, 128), F32),
            pltpu.VMEM((2, 2, s.RZ, 128), BF16),
            pltpu.VMEM((2, 2, steps, 2 * s.RZ, 128), BF16),
            pltpu.VMEM((2, 2 * s.RZ, 128), F32),
            pltpu.VMEM((X - 1, 2, 2 * s.RPD, 128), BF16),
            pltpu.VMEM((X - 1, 2, 2 * s.RPD, 128), BF16),
            pltpu.VMEM((2, 2 * s.RPD, 128), F32),
            pltpu.VMEM((2, s.RPD, 128), F32),
            pltpu.VMEM((YL, W, TOK), BF16),
            pltpu.VMEM((YL, W, TOK), BF16),
            pltpu.VMEM((YL, W, TOK), F32),
            pltpu.VMEM((YL, W, TOK), BF16),
            pltpu.VMEM((YL - 1, W, TOK), BF16),
            dma((2,)),
            dma((Z - 1,)),
            dma((Z - 1,)),
            dma((Q - 1,)),
            dma((Q - 1,)),
            dma((YL - 1,)),
            dma((YL - 1,)),
            dma((YL,)),
            dma((YL,)),
            dma((YL - 1,)),
            dma((YL - 1,)),
            dma((YL,)),
            dma((YL,)),
            dma((2, 2, steps)),
            dma((2, 2, steps)),
            dma((X - 1,)),
            dma((X - 1,)),
            dma,
            dma,
            dma,
            dma,
            dma((YL - 1,)),
            dma((YL - 1,)),
        ],
        compiler_params=pltpu.CompilerParams(
            collective_id=0, has_side_effects=True, vmem_limit_bytes=50 * 1024 * 1024
        ),
    )(
        loader_rows.T,
        pack_dest.reshape(1, TOK),
        segment_ids,
        jnp.transpose(w_qkv, (1, 2, 0)).reshape(3 * W, D),
        w_out,
        d_out.T,
        jnp.asarray(_regroup(s), BF16),
    )
    return grad, packed.T


def build(mesh, s):
    placed = (
        P("rep", "tp"),
        P("rep"),
        P("rep", None),
        P(None, None, "tp"),
        P("tp", None),
        P("rep", "tp"),
    )
    return jax.shard_map(
        functools.partial(shards, s),
        mesh=mesh,
        in_specs=placed,
        out_specs=(P("rep", "tp"), P("rep", "tp")),
        check_vma=False,
    )


def solution(mesh):
    return build(mesh, Sizes(2, 12, 4, 4, 2, 256, 224))
```

```python
import functools

import jax
import jax.numpy as jnp
from jax import lax
from jax.experimental import pallas as pl
from jax.experimental.pallas import tpu as pltpu
from jax.sharding import PartitionSpec as P

HEAD_DIM = 112
MESH = pl.DeviceIdType.MESH
F32 = jnp.float32
BF16 = jnp.bfloat16


def _dot(a, b, ca, cb):
    return lax.dot_general(a, b, (((ca,), (cb,)), ((), ())), preferred_element_type=F32)


def _nn(a, b):
    return _dot(a, b, 1, 0)


def _nt(a, b):
    return _dot(a, b, 1, 1)


def _tn(a, b):
    return _dot(a, b, 0, 0)


def _onehot(cond):
    return jnp.where(cond, 1.0, 0.0).astype(BF16)


class Copy:
    def __init__(self, *args, **kw):
        self.copy = pltpu.make_async_remote_copy(*args, **kw)
        self.copy.start()
        self.arrived = False

    def wait_recv(self):
        if not self.arrived:
            self.copy.wait_recv()
            self.arrived = True


class Sizes:
    def __init__(self, yh, z, x, yl, c, tok, width):
        self.YH, self.Z, self.X, self.YL, self.C = yh, z, x, yl, c
        self.TOK, self.W = tok, width
        self.R, self.T = yh * z * x, yl * c
        self.D = width * self.T
        self.Q = yh * x
        self.CAP = -(-tok // self.R)
        self.B1 = -(-self.Q * self.CAP // 16) * 16
        self.B2 = -(-self.Z * self.CAP // 16) * 16
        self.RPD = 3 * self.D // self.R
        self.RZ = x * self.RPD


def _kernel(
    s,
    ld, dest, seg, w_hbm, wo_hbm, cot,
    g_out, d_out,
    wv, wn, wo, s1, r1, s2, r2, xt, ct, dq3, f0, f1, a_stage0, a_stage1, a_slots0, a_slots1,
    b_s, b_r, b_f, b_stage0, b_stage1, b_slots0, b_slots1, red, xs, xr, acc, yr,
    ps_s, ps_r, pown, py_s, py_r,
    w_sem, z_ss, z_rs, q_ss, q_rs, cg_ss, cg_rs, cf_ss, cf_rs, xg_ss, xg_rs, xf_ss, xf_rs,
    a_ss, a_rs, b_ss, b_rs, bz_ss, bz_rs, x_ss, x_rs, y_ss, y_rs, pc_ss, pc_rs, py_ss, py_rs,
):
    W, TOK, Z, X, YH, YL, C, Q = s.W, s.TOK, s.Z, s.X, s.YH, s.YL, s.C, s.Q
    rep, tp = lax.axis_index("rep"), lax.axis_index("tp")
    mx = rep % X
    mz = (rep // X) % Z
    my = rep // (X * Z)
    ml, mc = tp // C, tp % C
    mq = my * X + mx

    def at_z(z):
        return {"rep": (my * Z + z) * X + mx}

    def at_q(q):
        return {"rep": ((q // X) * Z + mz) * X + q % X}

    def at_t(l, c):
        return {"tp": l * C + c}

    def rows(ref, start, size, unit):
        return ref.at[pl.ds(pl.multiple_of(start, unit), size)]

    def send(src, dst, ss, rs, device):
        copy = Copy(
            src_ref=src, dst_ref=dst, send_sem=ss, recv_sem=rs, device_id=device, device_id_type=MESH
        )
        started.append(copy)
        return copy

    def finish():
        for copy in started:
            copy.wait_recv()
            copy.copy.wait_send()

    started = []
    partners = [at_z((mz + o) % Z) for o in range(1, Z)]
    partners += [at_q((mq + o) % Q) for o in range(1, Q)]
    partners += [at_t((ml + o) % YL, mc) for o in range(1, YL)]
    partners += [at_t(ml, 1 - mc)]
    barrier = pltpu.get_barrier_semaphore()
    for device in partners:
        pl.semaphore_signal(barrier, inc=1, device_id=device, device_id_type=MESH)

    w_copy = pltpu.make_async_copy(w_hbm, wv, w_sem.at[0])
    w_copy.start()
    wo_copy = pltpu.make_async_copy(wo_hbm, wo, w_sem.at[1])
    wo_copy.start()

    dst = dest[...]
    pack, slot = dst // TOK, dst % TOK
    iota_p = lax.broadcasted_iota(jnp.int32, (128, TOK), 0)
    of_pack = _onehot(iota_p == pack)
    before = _onehot(
        lax.broadcasted_iota(jnp.int32, (TOK, TOK), 0) < lax.broadcasted_iota(jnp.int32, (TOK, TOK), 1)
    )
    rank = jnp.sum(_nn(of_pack, before) * of_pack.astype(F32), axis=0, keepdims=True).astype(jnp.int32)
    px, pz, py = pack % X, (pack // X) % Z, pack // (X * Z)
    place = pz * s.B1 + (py * X + px) * s.CAP + rank
    pick = _onehot(lax.broadcasted_iota(jnp.int32, (Z * s.B1, TOK), 0) == place)
    slot1 = jnp.broadcast_to((slot + 1).astype(F32), (256 - W, TOK)).astype(BF16)
    s1[...] = _nt(pick, jnp.concatenate([ld[...], slot1], axis=0)).astype(BF16)

    pl.semaphore_wait(barrier, len(partners))

    zc = []
    for o in range(1, Z):
        to = (mz + o) % Z
        zc.append(
            send(rows(s1, to * s.B1, s.B1, 16), rows(r1, mz * s.B1, s.B1, 16),
                 z_ss.at[o - 1], z_rs.at[o - 1], at_z(to))
        )
    r1[pl.ds(pl.multiple_of(mz * s.B1, 16), s.B1)] = s1[pl.ds(pl.multiple_of(mz * s.B1, 16), s.B1)]

    def gather(src, buf, ss, rs, fs, fr):
        mine = rows(buf, tp * W, W, 16)
        first = [send(src, mine, ss.at[o - 1], rs.at[o - 1], at_t((ml + o) % YL, mc)) for o in range(1, YL)]
        first.append(send(src, mine, fs.at[0], fr.at[0], at_t(ml, 1 - mc)))

        def rest():
            more = []
            for o in range(1, YL):
                first[o - 1].wait_recv()
                there = rows(buf, ((ml - o + YL) % YL * C + mc) * W, W, 16)
                more.append(send(there, there, fs.at[o], fr.at[o], at_t(ml, 1 - mc)))
            first[-1].wait_recv()
            for copy in more:
                copy.wait_recv()

        return rest

    cot_rest = gather(cot, ct, cg_ss, cg_rs, cf_ss, cf_rs)
    ct[pl.ds(pl.multiple_of(tp * W, 16), W)] = cot[...]

    w_copy.wait()
    for w in range(3):
        for j in range(0, s.D, 128):
            wn[w, pl.ds(j, 128)] = wv[pl.ds(w * W, W), pl.ds(j, 128)].T

    line = lax.broadcasted_iota(jnp.int32, (1, Z * s.B1), 1)
    inner = line % s.B1
    aim = inner // s.CAP * s.B2 + line // s.B1 * s.CAP + inner % s.CAP
    aim = jnp.where(inner < Q * s.CAP, aim, -1)
    regroup = _onehot(lax.broadcasted_iota(jnp.int32, (Q * s.B2, Z * s.B1), 0) == aim)
    for copy in zc:
        copy.wait_recv()
    s2[...] = _nn(regroup, r1[...]).astype(BF16)
    qc = []
    for o in range(1, Q):
        to = (mq + o) % Q
        qc.append(
            send(rows(s2, to * s.B2, s.B2, 16), rows(r2, mq * s.B2, s.B2, 16),
                 q_ss.at[o - 1], q_rs.at[o - 1], at_q(to))
        )
    r2[pl.ds(pl.multiple_of(mq * s.B2, 16), s.B2)] = s2[pl.ds(pl.multiple_of(mq * s.B2, 16), s.B2)]

    cot_rest()
    wo_copy.wait()
    d_attn = _nn(wo[...], ct[...]).astype(BF16)

    for copy in qc:
        copy.wait_recv()
    got = r2[...]
    slots_got = got[:, W:W + 1].astype(F32)
    iota_s = lax.broadcasted_iota(jnp.int32, (Q * s.B2, TOK), 1).astype(F32) + 1.0
    put = _onehot(slots_got == iota_s)
    xt[pl.ds(pl.multiple_of(tp * W, 16), W)] = _tn(got, put)[:W].astype(BF16)
    rows_rest = gather(rows(xt, tp * W, W, 16), xt, xg_ss, xg_rs, xf_ss, xf_rs)
    rows_rest()

    qkv = _nn(wv[...], xt[...]).astype(BF16)
    scale = HEAD_DIM ** (-0.5)
    seg_to = jnp.broadcast_to(seg[...].astype(F32), (TOK, TOK))
    same = seg_to.T == seg_to
    heads = W // HEAD_DIM
    for h in range(heads):
        lo = h * HEAD_DIM
        qt = qkv[lo:lo + HEAD_DIM]
        kt = qkv[W + lo:W + lo + HEAD_DIM]
        vt = qkv[2 * W + lo:2 * W + lo + HEAD_DIM]
        da = d_attn[lo:lo + HEAD_DIM]
        scores = jnp.where(same, _tn(kt, qt) * scale, -jnp.inf)
        expo = jnp.exp(scores - jnp.max(scores, axis=0, keepdims=True))
        probs = expo / jnp.sum(expo, axis=0, keepdims=True)
        probs_b = probs.astype(BF16)
        attn = _nn(vt, probs_b).astype(BF16)
        d_prob = _tn(vt, da)
        delta = jnp.sum(da.astype(F32) * attn.astype(F32), axis=0, keepdims=True)
        d_score = (probs * (d_prob - delta) * scale).astype(BF16)
        dq3[0, lo:lo + HEAD_DIM] = _nn(kt, d_score).astype(BF16)
        dq3[1, lo:lo + HEAD_DIM] = _nt(qt, d_score).astype(BF16)
        dq3[2, lo:lo + HEAD_DIM] = _nt(da, probs_b).astype(BF16)
    dq3[:, W:] = jnp.zeros((3, 256 - W, TOK), BF16)

    f = (f0, f1)
    a_stage, a_slots = (a_stage0, a_stage1), (a_slots0, a_slots1)
    b_stage, b_slots = (b_stage0, b_stage1), (b_slots0, b_slots1)
    for t in range(s.T):
        block = xt[t * W:(t + 1) * W]
        for w in range(3):
            g = _nt(block, dq3[w])
            for h in range(2):
                f[h][pl.ds(t * 3 * W + w, W, stride=3)] = g[:, h * 128:(h + 1) * 128]

    def chunk(h, y, z, x, size):
        return f[h][pl.ds(pl.multiple_of(((y * Z + z) * X + x) * s.RPD, 8), size)]

    def rel(off):
        return (mz + off + Z) % Z

    steps = Z // 2

    class Ring:
        def __init__(self, own, stage, slots, ss, rs):
            self.own, self.stage, self.slots, self.ss, self.rs = own, stage, slots, ss, rs
            self.copies = {}

        def step(self, k):
            for i in range(2):
                for d in range(2):
                    p = (d + i) % 2
                    sign = 1 if d == 0 else -1
                    if k == 1 and p != d:
                        continue
                    off = sign * (steps + 1 - k)
                    term = self.own(p, off)
                    first = k == (1 if p == d else 2)
                    if first:
                        src = self.stage[p].at[d]
                    else:
                        self.copies[d, p, k - 1].wait_recv()
                        src = self.slots[p].at[d, k - 2]
                        term = term + src[...].astype(F32)
                    src[...] = term.astype(BF16)
                    self.copies[d, p, k] = send(
                        src, self.slots[p].at[d, k - 1], self.ss.at[d, p, k - 1], self.rs.at[d, p, k - 1],
                        at_z(rel(sign)),
                    )

        def total(self, p):
            value = self.own(p, 0)
            for d in range(2):
                self.copies[d, p, steps].wait_recv()
                value = value + self.slots[p][d, steps - 1].astype(F32)
            return value

    offs = [steps]
    for k in range(steps - 1, 0, -1):
        offs += [k, -k]
    offs += [0]
    cuts = [0, min(5, len(offs) - 1), len(offs)]
    two = 2 * s.RPD

    def of_x(h, off, x):
        return jnp.concatenate([chunk(h, y, rel(off), x, s.RPD) for y in range(YH)], axis=0)

    b_copies = {}

    def b_send(piece):
        lo, hi = cuts[piece], cuts[piece + 1]
        for o in range(1, X):
            to = (mx + o) % X
            for i in range(lo, hi):
                b_s[o - 1, i * two:(i + 1) * two] = of_x(1, offs[i], to).astype(BF16)
            span = pl.ds(lo * two, (hi - lo) * two)
            b_copies[piece, o] = send(b_s.at[o - 1, span], b_r.at[o - 1, span],
                                      b_ss.at[o - 1, piece], b_rs.at[o - 1, piece], at_q(my * X + to))

    def b_sum(piece):
        for o in range(1, X):
            b_copies[piece, o].wait_recv()
        for i in range(cuts[piece], cuts[piece + 1]):
            value = of_x(1, offs[i], mx)
            for o in range(1, X):
                value = value + b_r[o - 1, i * two:(i + 1) * two].astype(F32)
            b_f[i] = value

    half = -(-s.RPD // 16) * 16
    ends = (0, half, two)
    ring_a = Ring(lambda p, off: chunk(0, p, rel(off), 0, s.RZ), a_stage, a_slots, a_ss, a_rs)
    ring_b = Ring(
        lambda p, off: b_f[offs.index(off) if off in offs else 0, ends[p]:ends[p + 1]],
        b_stage, b_slots, bz_ss, bz_rs,
    )

    def part(t):
        t = pl.multiple_of(t * W, 16)
        total = _nn(wn[0, pl.ds(t, W)], dq3[0, :W])
        total += _nn(wn[1, pl.ds(t, W)], dq3[1, :W])
        return total + _nn(wn[2, pl.ds(t, W)], dq3[2, :W])

    b_send(0)
    ring_a.step(1)
    b_send(1)
    for l in range(YL):
        ps_s[l] = part(l * C + 1 - mc).astype(BF16)
    pair = send(ps_s, ps_r, pc_ss, pc_rs, at_t(ml, 1 - mc))
    ring_a.step(2)
    for l in range(YL):
        pown[l] = part(l * C + mc)
    b_sum(0)
    ring_b.step(1)
    if steps >= 3:
        ring_a.step(3)
    pair.wait_recv()
    for l in range(YL):
        pown[l] = pown[l] + ps_r[l].astype(F32)
        py_s[l] = pown[l].astype(BF16)
    pc = []
    for o in range(1, YL):
        to = (ml + o) % YL
        pc.append(send(py_s.at[to], py_r.at[o - 1], py_ss.at[o - 1], py_rs.at[o - 1], at_t(to, mc)))
    ring_b.step(2)
    b_sum(1)
    for k in range(4, steps + 1):
        ring_a.step(k)
        ring_b.step(k - 1)
    for k in range(max(3, steps), steps + 1):
        ring_b.step(k)
    for y in range(YH):
        red[y * s.RZ:(y + 1) * s.RZ] = ring_a.total(y)

    def red_x(x):
        return jnp.concatenate(
            [red[pl.ds(pl.multiple_of(y * s.RZ + x * s.RPD, 8), s.RPD)] for y in range(YH)], axis=0
        )

    xc = []
    for o in range(1, X):
        to = (mx + o) % X
        xs[o - 1] = red_x(to).astype(BF16)
        xc.append(send(xs.at[o - 1], xr.at[o - 1], x_ss.at[o - 1], x_rs.at[o - 1], at_q(my * X + to)))

    for copy in pc:
        copy.wait_recv()
    total = pown[ml]
    for o in range(1, YL):
        total = total + py_r[o - 1].astype(F32)
    d_out[...] = total.astype(BF16)

    for p in range(2):
        acc[1, ends[p]:ends[p + 1]] = ring_b.total(p)
    value = red_x(mx)
    for o in range(1, X):
        xc[o - 1].wait_recv()
        value = value + xr[o - 1].astype(F32)
    acc[0] = value

    other = 1 - my
    yc = send(acc.at[:, pl.ds(pl.multiple_of(other * s.RPD, 8), s.RPD)], yr, y_ss, y_rs, at_q(other * X + mx))
    yc.wait_recv()
    norm = (TOK * s.R) ** (-0.5)
    mine = pl.ds(pl.multiple_of(my * s.RPD, 8), s.RPD)
    g_out[:, :128] = (acc[0, mine] + yr[0]) * norm
    g_out[:, 128:] = ((acc[1, mine] + yr[1]) * norm)[:, :W - 128]

    finish()


def shards(s, loader_rows, pack_dest, segment_ids, w_qkv, w_out, d_out):
    W, TOK, D = s.W, s.TOK, s.D
    Q, Z, X, YL = s.Q, s.Z, s.X, s.YL
    dma = pltpu.SemaphoreType.DMA
    vmem = pl.BlockSpec(memory_space=pltpu.VMEM)
    hbm = pl.BlockSpec(memory_space=pl.ANY)
    steps = Z // 2
    two, half = 2 * s.RPD, -(-s.RPD // 16) * 16
    grad, packed = pl.pallas_call(
        functools.partial(_kernel, s),
        out_shape=(
            jax.ShapeDtypeStruct((s.RPD, W), F32),
            jax.ShapeDtypeStruct((W, TOK), BF16),
        ),
        in_specs=[vmem, vmem, vmem, hbm, hbm, vmem],
        out_specs=(vmem, vmem),
        scratch_shapes=[
            pltpu.VMEM((3 * W, D), BF16),
            pltpu.VMEM((3, D, W), BF16),
            pltpu.VMEM((W, D), BF16),
            pltpu.VMEM((Z * s.B1, 256), BF16),
            pltpu.VMEM((Z * s.B1, 256), BF16),
            pltpu.VMEM((Q * s.B2, 256), BF16),
            pltpu.VMEM((Q * s.B2, 256), BF16),
            pltpu.VMEM((D, TOK), BF16),
            pltpu.VMEM((D, TOK), BF16),
            pltpu.VMEM((3, 256, TOK), BF16),
            pltpu.VMEM((3 * D, 128), F32),
            pltpu.VMEM((3 * D, 128), F32),
            pltpu.VMEM((2, s.RZ, 128), BF16),
            pltpu.VMEM((2, s.RZ, 128), BF16),
            pltpu.VMEM((2, steps, s.RZ, 128), BF16),
            pltpu.VMEM((2, steps, s.RZ, 128), BF16),
            pltpu.VMEM((X - 1, Z * two, 128), BF16),
            pltpu.VMEM((X - 1, Z * two, 128), BF16),
            pltpu.VMEM((Z, two, 128), F32),
            pltpu.VMEM((2, half, 128), BF16),
            pltpu.VMEM((2, two - half, 128), BF16),
            pltpu.VMEM((2, steps, half, 128), BF16),
            pltpu.VMEM((2, steps, two - half, 128), BF16),
            pltpu.VMEM((2 * s.RZ, 128), F32),
            pltpu.VMEM((X - 1, two, 128), BF16),
            pltpu.VMEM((X - 1, two, 128), BF16),
            pltpu.VMEM((2, 2 * s.RPD, 128), F32),
            pltpu.VMEM((2, s.RPD, 128), F32),
            pltpu.VMEM((YL, W, TOK), BF16),
            pltpu.VMEM((YL, W, TOK), BF16),
            pltpu.VMEM((YL, W, TOK), F32),
            pltpu.VMEM((YL, W, TOK), BF16),
            pltpu.VMEM((YL - 1, W, TOK), BF16),
            dma((2,)),
            dma((Z - 1,)),
            dma((Z - 1,)),
            dma((Q - 1,)),
            dma((Q - 1,)),
            dma((YL - 1,)),
            dma((YL - 1,)),
            dma((YL,)),
            dma((YL,)),
            dma((YL - 1,)),
            dma((YL - 1,)),
            dma((YL,)),
            dma((YL,)),
            dma((2, 2, steps)),
            dma((2, 2, steps)),
            dma((X - 1, 2)),
            dma((X - 1, 2)),
            dma((2, 2, steps)),
            dma((2, 2, steps)),
            dma((X - 1,)),
            dma((X - 1,)),
            dma,
            dma,
            dma,
            dma,
            dma((YL - 1,)),
            dma((YL - 1,)),
        ],
        compiler_params=pltpu.CompilerParams(
            collective_id=0, has_side_effects=True, vmem_limit_bytes=60 * 1024 * 1024
        ),
    )(
        loader_rows.T,
        pack_dest.reshape(1, TOK),
        segment_ids,
        jnp.transpose(w_qkv, (1, 2, 0)).reshape(3 * W, D),
        w_out,
        d_out.T,
    )
    return grad, packed.T


def build(mesh, s):
    placed = (
        P("rep", "tp"),
        P("rep"),
        P("rep", None),
        P(None, None, "tp"),
        P("tp", None),
        P("rep", "tp"),
    )
    return jax.shard_map(
        functools.partial(shards, s),
        mesh=mesh,
        in_specs=placed,
        out_specs=(P("rep", "tp"), P("rep", "tp")),
        check_vma=False,
    )


def solution(mesh):
    return build(mesh, Sizes(2, 12, 4, 4, 2, 256, 224))
```

```python
import functools

import jax
import jax.numpy as jnp
from jax import lax
from jax.experimental import pallas as pl
from jax.experimental.pallas import tpu as pltpu
from jax.sharding import PartitionSpec as P

HEAD_DIM = 112
A_PARTS = 4
MESH = pl.DeviceIdType.MESH
F32 = jnp.float32
BF16 = jnp.bfloat16


def _dot(a, b, ca, cb):
    return lax.dot_general(a, b, (((ca,), (cb,)), ((), ())), preferred_element_type=F32)


def _nn(a, b):
    return _dot(a, b, 1, 0)


def _nt(a, b):
    return _dot(a, b, 1, 1)


def _tn(a, b):
    return _dot(a, b, 0, 0)


def _onehot(cond):
    return jnp.where(cond, 1.0, 0.0).astype(BF16)


class Copy:
    def __init__(self, *args, **kw):
        self.copy = pltpu.make_async_remote_copy(*args, **kw)
        self.copy.start()
        self.arrived = False

    def wait_recv(self):
        if not self.arrived:
            self.copy.wait_recv()
            self.arrived = True


class Sizes:
    def __init__(self, yh, z, x, yl, c, tok, width):
        self.YH, self.Z, self.X, self.YL, self.C = yh, z, x, yl, c
        self.TOK, self.W = tok, width
        self.R, self.T = yh * z * x, yl * c
        self.D = width * self.T
        self.Q = yh * x
        self.CAP = -(-tok // self.R)
        self.B1 = -(-self.Q * self.CAP // 16) * 16
        self.B2 = -(-self.Z * self.CAP // 16) * 16
        self.RPD = 3 * self.D // self.R
        self.RZ = x * self.RPD


def _kernel(
    s,
    ld, dest, seg, w_hbm, wo_hbm, cot,
    g_out, d_out,
    wv, wn, wo, s1, r1, s2, r2, xt, ct, dq3, f0, f1, a_stage, a_slots,
    b_s, b_r, b_f, b_stage, b_slots, red, xs, xr, acc, yr,
    ps_s, ps_r, pown, py_s, py_r,
    w_sem, z_ss, z_rs, q_ss, q_rs, cg_ss, cg_rs, cf_ss, cf_rs, xg_ss, xg_rs, xf_ss, xf_rs,
    a_ss, a_rs, b_ss, b_rs, bz_ss, bz_rs, x_ss, x_rs, y_ss, y_rs, pc_ss, pc_rs, py_ss, py_rs,
):
    W, TOK, Z, X, YH, YL, C, Q = s.W, s.TOK, s.Z, s.X, s.YH, s.YL, s.C, s.Q
    rep, tp = lax.axis_index("rep"), lax.axis_index("tp")
    mx = rep % X
    mz = (rep // X) % Z
    my = rep // (X * Z)
    ml, mc = tp // C, tp % C
    mq = my * X + mx

    def at_z(z):
        return {"rep": (my * Z + z) * X + mx}

    def at_q(q):
        return {"rep": ((q // X) * Z + mz) * X + q % X}

    def at_t(l, c):
        return {"tp": l * C + c}

    def rows(ref, start, size, unit):
        return ref.at[pl.ds(pl.multiple_of(start, unit), size)]

    def send(src, dst, ss, rs, device):
        copy = Copy(
            src_ref=src, dst_ref=dst, send_sem=ss, recv_sem=rs, device_id=device, device_id_type=MESH
        )
        started.append(copy)
        return copy

    def finish():
        for copy in started:
            copy.wait_recv()
            copy.copy.wait_send()

    started = []
    partners = [at_z((mz + o) % Z) for o in range(1, Z)]
    partners += [at_q((mq + o) % Q) for o in range(1, Q)]
    partners += [at_t((ml + o) % YL, mc) for o in range(1, YL)]
    partners += [at_t(ml, 1 - mc)]
    barrier = pltpu.get_barrier_semaphore()
    for device in partners:
        pl.semaphore_signal(barrier, inc=1, device_id=device, device_id_type=MESH)

    w_copy = pltpu.make_async_copy(w_hbm, wv, w_sem.at[0])
    w_copy.start()
    wo_copy = pltpu.make_async_copy(wo_hbm, wo, w_sem.at[1])
    wo_copy.start()

    dst = dest[...]
    pack, slot = dst // TOK, dst % TOK
    iota_p = lax.broadcasted_iota(jnp.int32, (128, TOK), 0)
    of_pack = _onehot(iota_p == pack)
    before = _onehot(
        lax.broadcasted_iota(jnp.int32, (TOK, TOK), 0) < lax.broadcasted_iota(jnp.int32, (TOK, TOK), 1)
    )
    rank = jnp.sum(_nn(of_pack, before) * of_pack.astype(F32), axis=0, keepdims=True).astype(jnp.int32)
    px, pz, py = pack % X, (pack // X) % Z, pack // (X * Z)
    place = pz * s.B1 + (py * X + px) * s.CAP + rank
    pick = _onehot(lax.broadcasted_iota(jnp.int32, (Z * s.B1, TOK), 0) == place)
    slot1 = jnp.broadcast_to((slot + 1).astype(F32), (256 - W, TOK)).astype(BF16)
    s1[...] = _nt(pick, jnp.concatenate([ld[...], slot1], axis=0)).astype(BF16)

    pl.semaphore_wait(barrier, len(partners))

    zc = []
    for o in range(1, Z):
        to = (mz + o) % Z
        zc.append(
            send(rows(s1, to * s.B1, s.B1, 16), rows(r1, mz * s.B1, s.B1, 16),
                 z_ss.at[o - 1], z_rs.at[o - 1], at_z(to))
        )
    r1[pl.ds(pl.multiple_of(mz * s.B1, 16), s.B1)] = s1[pl.ds(pl.multiple_of(mz * s.B1, 16), s.B1)]

    def gather(src, buf, ss, rs, fs, fr):
        mine = rows(buf, tp * W, W, 16)
        first = [send(src, mine, ss.at[o - 1], rs.at[o - 1], at_t((ml + o) % YL, mc)) for o in range(1, YL)]
        first.append(send(src, mine, fs.at[0], fr.at[0], at_t(ml, 1 - mc)))

        def rest():
            more = []
            for o in range(1, YL):
                first[o - 1].wait_recv()
                there = rows(buf, ((ml - o + YL) % YL * C + mc) * W, W, 16)
                more.append(send(there, there, fs.at[o], fr.at[o], at_t(ml, 1 - mc)))
            first[-1].wait_recv()
            for copy in more:
                copy.wait_recv()

        return rest

    cot_rest = gather(cot, ct, cg_ss, cg_rs, cf_ss, cf_rs)
    ct[pl.ds(pl.multiple_of(tp * W, 16), W)] = cot[...]

    w_copy.wait()
    for w in range(3):
        for j in range(0, s.D, 128):
            wn[w, pl.ds(j, 128)] = wv[pl.ds(w * W, W), pl.ds(j, 128)].T

    line = lax.broadcasted_iota(jnp.int32, (1, Z * s.B1), 1)
    inner = line % s.B1
    aim = inner // s.CAP * s.B2 + line // s.B1 * s.CAP + inner % s.CAP
    aim = jnp.where(inner < Q * s.CAP, aim, -1)
    regroup = _onehot(lax.broadcasted_iota(jnp.int32, (Q * s.B2, Z * s.B1), 0) == aim)
    for copy in zc:
        copy.wait_recv()
    s2[...] = _nn(regroup, r1[...]).astype(BF16)
    qc = []
    for o in range(1, Q):
        to = (mq + o) % Q
        qc.append(
            send(rows(s2, to * s.B2, s.B2, 16), rows(r2, mq * s.B2, s.B2, 16),
                 q_ss.at[o - 1], q_rs.at[o - 1], at_q(to))
        )
    r2[pl.ds(pl.multiple_of(mq * s.B2, 16), s.B2)] = s2[pl.ds(pl.multiple_of(mq * s.B2, 16), s.B2)]

    cot_rest()
    wo_copy.wait()
    d_attn = _nn(wo[...], ct[...]).astype(BF16)

    for copy in qc:
        copy.wait_recv()
    got = r2[...]
    slots_got = got[:, W:W + 1].astype(F32)
    iota_s = lax.broadcasted_iota(jnp.int32, (Q * s.B2, TOK), 1).astype(F32) + 1.0
    put = _onehot(slots_got == iota_s)
    xt[pl.ds(pl.multiple_of(tp * W, 16), W)] = _tn(got, put)[:W].astype(BF16)
    rows_rest = gather(rows(xt, tp * W, W, 16), xt, xg_ss, xg_rs, xf_ss, xf_rs)
    rows_rest()

    qkv = _nn(wv[...], xt[...]).astype(BF16)
    scale = HEAD_DIM ** (-0.5)
    seg_to = jnp.broadcast_to(seg[...].astype(F32), (TOK, TOK))
    same = seg_to.T == seg_to
    heads = W // HEAD_DIM
    for h in range(heads):
        lo = h * HEAD_DIM
        qt = qkv[lo:lo + HEAD_DIM]
        kt = qkv[W + lo:W + lo + HEAD_DIM]
        vt = qkv[2 * W + lo:2 * W + lo + HEAD_DIM]
        da = d_attn[lo:lo + HEAD_DIM]
        scores = jnp.where(same, _tn(kt, qt) * scale, -jnp.inf)
        expo = jnp.exp(scores - jnp.max(scores, axis=0, keepdims=True))
        probs = expo / jnp.sum(expo, axis=0, keepdims=True)
        probs_b = probs.astype(BF16)
        attn = _nn(vt, probs_b).astype(BF16)
        d_prob = _tn(vt, da)
        delta = jnp.sum(da.astype(F32) * attn.astype(F32), axis=0, keepdims=True)
        d_score = (probs * (d_prob - delta) * scale).astype(BF16)
        dq3[0, lo:lo + HEAD_DIM] = _nn(kt, d_score).astype(BF16)
        dq3[1, lo:lo + HEAD_DIM] = _nt(qt, d_score).astype(BF16)
        dq3[2, lo:lo + HEAD_DIM] = _nt(da, probs_b).astype(BF16)
    dq3[:, W:] = jnp.zeros((3, 256 - W, TOK), BF16)

    f = (f0, f1)
    for t in range(s.T):
        block = xt[t * W:(t + 1) * W]
        for w in range(3):
            g = _nt(block, dq3[w])
            for h in range(2):
                f[h][pl.ds(t * 3 * W + w, W, stride=3)] = g[:, h * 128:(h + 1) * 128]

    def chunk(h, y, z, x, size):
        return f[h][pl.ds(pl.multiple_of(((y * Z + z) * X + x) * s.RPD, 8), size)]

    def rel(off):
        return (mz + off + Z) % Z

    steps = Z // 2

    a_len = YH * s.RZ // A_PARTS

    def a_own(p, off):
        per_y = A_PARTS // YH
        start = (p // per_y * Z + rel(off)) * s.RZ + p % per_y * a_len
        return f0[pl.ds(pl.multiple_of(start, 8), a_len)]

    a_copies = {}

    def a_step(k):
        for i in range(A_PARTS):
            for d in range(2):
                p = (i + d * A_PARTS // 2) % A_PARTS
                owner = p * 2 // A_PARTS
                if k == 1 and owner != d:
                    continue
                sign = 1 if d == 0 else -1
                term = a_own(p, sign * (steps + 1 - k))
                if k == (1 if owner == d else 2):
                    src = a_stage.at[p, d]
                else:
                    a_copies[d, p, k - 1].wait_recv()
                    src = a_slots.at[d, p, k - 2]
                    term = term + src[...].astype(F32)
                src[...] = term.astype(BF16)
                a_copies[d, p, k] = send(
                    src, a_slots.at[d, p, k - 1], a_ss.at[d, p, k - 1], a_rs.at[d, p, k - 1], at_z(rel(sign))
                )

    def a_total(p):
        value = a_own(p, 0)
        for d in range(2):
            a_copies[d, p, steps].wait_recv()
            value = value + a_slots[d, p, steps - 1].astype(F32)
        return value

    offs = [steps]
    cuts = [0, 1]
    for k in range(steps - 1, 0, -1):
        offs += [k, -k]
        cuts += [len(offs)]
    offs += [0]
    cuts += [len(offs)]
    two = 2 * s.RPD

    def of_x(h, off, x):
        return jnp.concatenate([chunk(h, y, rel(off), x, s.RPD) for y in range(YH)], axis=0)

    b_copies = {}

    def b_send(piece):
        lo, hi = cuts[piece], cuts[piece + 1]
        for o in range(1, X):
            to = (mx + o) % X
            for i in range(lo, hi):
                b_s[o - 1, i * two:(i + 1) * two] = of_x(1, offs[i], to).astype(BF16)
            span = pl.ds(lo * two, (hi - lo) * two)
            b_copies[piece, o] = send(b_s.at[o - 1, span], b_r.at[o - 1, span],
                                      b_ss.at[o - 1, piece], b_rs.at[o - 1, piece], at_q(my * X + to))

    def b_sum(piece):
        for o in range(1, X):
            b_copies[piece, o].wait_recv()
        for i in range(cuts[piece], cuts[piece + 1]):
            value = of_x(1, offs[i], mx)
            for o in range(1, X):
                value = value + b_r[o - 1, i * two:(i + 1) * two].astype(F32)
            b_f[i] = value

    half = -(-s.RPD // 16) * 16
    ends = (0, half, two)
    b_ring = {}

    def b_step(k):
        b_sum(k - 1)
        for d in range(2):
            sign = 1 if d == 0 else -1
            i = offs.index(sign * (steps + 1 - k)) if k > 1 else 0
            span = pl.ds(ends[d], ends[d + 1] - ends[d])
            if k == 1:
                b_stage[span] = b_f[i, span].astype(BF16)
                src, dst = b_stage.at[span], b_slots.at[d, 0, span]
            else:
                b_ring[d, k - 1].wait_recv()
                if k == 2:
                    b_f[i, span] = b_f[i, span] + b_slots[d, 0, span].astype(F32)
                    b_slots[d, 0] = b_f[i].astype(BF16)
                else:
                    b_slots[d, k - 2] = (b_f[i] + b_slots[d, k - 2].astype(F32)).astype(BF16)
                src, dst = b_slots.at[d, k - 2], b_slots.at[d, k - 1]
            b_ring[d, k] = send(src, dst, bz_ss.at[d, k - 1], bz_rs.at[d, k - 1], at_z(rel(sign)))

    def part(t):
        t = pl.multiple_of(t * W, 16)
        total = _nn(wn[0, pl.ds(t, W)], dq3[0, :W])
        total += _nn(wn[1, pl.ds(t, W)], dq3[1, :W])
        return total + _nn(wn[2, pl.ds(t, W)], dq3[2, :W])

    for piece in range(2):
        b_send(piece)
    a_step(1)
    for piece in range(2, len(cuts) - 1):
        b_send(piece)
    for l in range(YL):
        ps_s[l] = part(l * C + 1 - mc).astype(BF16)
    pair = send(ps_s, ps_r, pc_ss, pc_rs, at_t(ml, 1 - mc))
    b_step(1)
    a_step(2)
    for l in range(YL):
        pown[l] = part(l * C + mc)
    pair.wait_recv()
    for l in range(YL):
        pown[l] = pown[l] + ps_r[l].astype(F32)
        py_s[l] = pown[l].astype(BF16)
    pc = []
    for o in range(1, YL):
        to = (ml + o) % YL
        pc.append(send(py_s.at[to], py_r.at[o - 1], py_ss.at[o - 1], py_rs.at[o - 1], at_t(to, mc)))
    for k in range(2, steps + 1):
        b_step(k)
        if k < steps:
            a_step(k + 1)
    b_sum(steps)
    value = b_f[len(offs) - 1]
    for d in range(2):
        b_ring[d, steps].wait_recv()
        value = value + b_slots[d, steps - 1].astype(F32)
    acc[...] = value
    other = 1 - my
    yc = send(acc.at[pl.ds(pl.multiple_of(other * s.RPD, 8), s.RPD)], yr, y_ss, y_rs, at_q(other * X + mx))

    for p in range(A_PARTS):
        red[p * a_len:(p + 1) * a_len] = a_total(p)

    def red_q(q):
        return red[pl.ds(pl.multiple_of(q * s.RPD, 8), s.RPD)]

    fill = jnp.zeros((xs.shape[1] - s.RPD, 128), F32)
    xc = []
    for o in range(1, Q):
        to = (mq + o) % Q
        xs[o - 1] = jnp.concatenate([red_q(to), fill], axis=0).astype(BF16)
        xc.append(send(xs.at[o - 1], xr.at[o - 1], x_ss.at[o - 1], x_rs.at[o - 1], at_q(to)))

    for copy in pc:
        copy.wait_recv()
    total = pown[ml]
    for o in range(1, YL):
        total = total + py_r[o - 1].astype(F32)
    d_out[...] = total.astype(BF16)

    value = red_q(mq)
    for o in range(1, Q):
        xc[o - 1].wait_recv()
        value = value + xr[o - 1, :s.RPD].astype(F32)
    yc.wait_recv()
    norm = (TOK * s.R) ** (-0.5)
    mine = pl.ds(pl.multiple_of(my * s.RPD, 8), s.RPD)
    g_out[:, :128] = value * norm
    g_out[:, 128:] = ((acc[mine] + yr[...]) * norm)[:, :W - 128]

    finish()


def shards(s, loader_rows, pack_dest, segment_ids, w_qkv, w_out, d_out):
    W, TOK, D = s.W, s.TOK, s.D
    Q, Z, X, YL = s.Q, s.Z, s.X, s.YL
    dma = pltpu.SemaphoreType.DMA
    vmem = pl.BlockSpec(memory_space=pltpu.VMEM)
    hbm = pl.BlockSpec(memory_space=pl.ANY)
    steps = Z // 2
    two = 2 * s.RPD
    grad, packed = pl.pallas_call(
        functools.partial(_kernel, s),
        out_shape=(
            jax.ShapeDtypeStruct((s.RPD, W), F32),
            jax.ShapeDtypeStruct((W, TOK), BF16),
        ),
        in_specs=[vmem, vmem, vmem, hbm, hbm, vmem],
        out_specs=(vmem, vmem),
        scratch_shapes=[
            pltpu.VMEM((3 * W, D), BF16),
            pltpu.VMEM((3, D, W), BF16),
            pltpu.VMEM((W, D), BF16),
            pltpu.VMEM((Z * s.B1, 256), BF16),
            pltpu.VMEM((Z * s.B1, 256), BF16),
            pltpu.VMEM((Q * s.B2, 256), BF16),
            pltpu.VMEM((Q * s.B2, 256), BF16),
            pltpu.VMEM((D, TOK), BF16),
            pltpu.VMEM((D, TOK), BF16),
            pltpu.VMEM((3, 256, TOK), BF16),
            pltpu.VMEM((3 * D, 128), F32),
            pltpu.VMEM((3 * D, 128), F32),
            pltpu.VMEM((A_PARTS, 2, 2 * s.RZ // A_PARTS, 128), BF16),
            pltpu.VMEM((2, A_PARTS, steps, 2 * s.RZ // A_PARTS, 128), BF16),
            pltpu.VMEM((X - 1, Z * two, 128), BF16),
            pltpu.VMEM((X - 1, Z * two, 128), BF16),
            pltpu.VMEM((Z, two, 128), F32),
            pltpu.VMEM((two, 128), BF16),
            pltpu.VMEM((2, steps, two, 128), BF16),
            pltpu.VMEM((2 * s.RZ, 128), F32),
            pltpu.VMEM((Q - 1, -(-s.RPD // 16) * 16, 128), BF16),
            pltpu.VMEM((Q - 1, -(-s.RPD // 16) * 16, 128), BF16),
            pltpu.VMEM((2 * s.RPD, 128), F32),
            pltpu.VMEM((s.RPD, 128), F32),
            pltpu.VMEM((YL, W, TOK), BF16),
            pltpu.VMEM((YL, W, TOK), BF16),
            pltpu.VMEM((YL, W, TOK), F32),
            pltpu.VMEM((YL, W, TOK), BF16),
            pltpu.VMEM((YL - 1, W, TOK), BF16),
            dma((2,)),
            dma((Z - 1,)),
            dma((Z - 1,)),
            dma((Q - 1,)),
            dma((Q - 1,)),
            dma((YL,)),
            dma((YL,)),
            dma((YL,)),
            dma((YL,)),
            dma((YL,)),
            dma((YL,)),
            dma((YL,)),
            dma((YL,)),
            dma((2, A_PARTS, steps)),
            dma((2, A_PARTS, steps)),
            dma((X - 1, steps + 1)),
            dma((X - 1, steps + 1)),
            dma((2, steps)),
            dma((2, steps)),
            dma((Q - 1,)),
            dma((Q - 1,)),
            dma,
            dma,
            dma,
            dma,
            dma((YL - 1,)),
            dma((YL - 1,)),
        ],
        compiler_params=pltpu.CompilerParams(
            collective_id=0, has_side_effects=True, vmem_limit_bytes=60 * 1024 * 1024
        ),
    )(
        loader_rows.T,
        pack_dest.reshape(1, TOK),
        segment_ids,
        jnp.transpose(w_qkv, (1, 2, 0)).reshape(3 * W, D),
        w_out,
        d_out.T,
    )
    return grad, packed.T


def build(mesh, s):
    placed = (
        P("rep", "tp"),
        P("rep"),
        P("rep", None),
        P(None, None, "tp"),
        P("tp", None),
        P("rep", "tp"),
    )
    return jax.shard_map(
        functools.partial(shards, s),
        mesh=mesh,
        in_specs=placed,
        out_specs=(P("rep", "tp"), P("rep", "tp")),
        check_vma=False,
    )


def solution(mesh):
    return build(mesh, Sizes(2, 12, 4, 4, 2, 256, 224))
```

```python
import functools

import jax
import jax.numpy as jnp
from jax import lax
from jax.experimental import pallas as pl
from jax.experimental.pallas import tpu as pltpu
from jax.sharding import PartitionSpec as P

HEAD_DIM = 112
A_PARTS = 4
MESH = pl.DeviceIdType.MESH
F32 = jnp.float32
BF16 = jnp.bfloat16


def _dot(a, b, ca, cb):
    return lax.dot_general(a, b, (((ca,), (cb,)), ((), ())), preferred_element_type=F32)


def _nn(a, b):
    return _dot(a, b, 1, 0)


def _nt(a, b):
    return _dot(a, b, 1, 1)


def _tn(a, b):
    return _dot(a, b, 0, 0)


def _onehot(cond):
    return jnp.where(cond, 1.0, 0.0).astype(BF16)


class Copy:
    def __init__(self, *args, **kw):
        self.copy = pltpu.make_async_remote_copy(*args, **kw)
        self.copy.start()
        self.arrived = False
        self.left = False

    def wait_recv(self):
        if not self.arrived:
            self.copy.wait_recv()
            self.arrived = True

    def wait_send(self):
        if not self.left:
            self.copy.wait_send()
            self.left = True


class Sizes:
    def __init__(self, yh, z, x, yl, c, tok, width):
        self.YH, self.Z, self.X, self.YL, self.C = yh, z, x, yl, c
        self.TOK, self.W = tok, width
        self.R, self.T = yh * z * x, yl * c
        self.D = width * self.T
        self.Q = yh * x
        self.CAP = -(-tok // self.R)
        self.B1 = -(-self.Q * self.CAP // 16) * 16
        self.B2 = -(-self.Z * self.CAP // 16) * 16
        self.RPD = 3 * self.D // self.R
        self.RZ = x * self.RPD


def _kernel(
    s,
    ld, dest, seg, w_hbm, wo_hbm, cot,
    g_out, d_out,
    wv, wn, wo, s1, r1, s2, r2, xt, ct, dq3, f0, f1, a_stage, a_slots,
    b_s, b_r, b_f, b_stage, b_slots, red, xs, xr, acc, yr,
    ps_s, ps_r, pown, py_s, py_r,
    w_sem, z_ss, z_rs, q_ss, q_rs, cg_ss, cg_rs, cf_ss, cf_rs, xg_ss, xg_rs, xf_ss, xf_rs,
    a_ss, a_rs, b_ss, b_rs, bz_ss, bz_rs, x_ss, x_rs, y_ss, y_rs, pc_ss, pc_rs, py_ss, py_rs,
):
    W, TOK, Z, X, YH, YL, C, Q = s.W, s.TOK, s.Z, s.X, s.YH, s.YL, s.C, s.Q
    rep, tp = lax.axis_index("rep"), lax.axis_index("tp")
    mx = rep % X
    mz = (rep // X) % Z
    my = rep // (X * Z)
    ml, mc = tp // C, tp % C
    mq = my * X + mx

    def at_z(z):
        return {"rep": (my * Z + z) * X + mx}

    def at_q(q):
        return {"rep": ((q // X) * Z + mz) * X + q % X}

    def at_t(l, c):
        return {"tp": l * C + c}

    def rows(ref, start, size, unit):
        return ref.at[pl.ds(pl.multiple_of(start, unit), size)]

    def send(src, dst, ss, rs, device):
        copy = Copy(
            src_ref=src, dst_ref=dst, send_sem=ss, recv_sem=rs, device_id=device, device_id_type=MESH
        )
        started.append(copy)
        return copy

    def settle():
        for copy in started:
            if copy.arrived:
                copy.wait_send()

    def finish():
        for copy in started:
            copy.wait_recv()
            copy.wait_send()

    others = [(dy, dx) for dy in range(YH - 1, -1, -1) for dx in range(X) if dy or dx]

    def q_of(o):
        dy, dx = others[o - 1]
        return (my + dy) % YH * X + (mx + dx) % X

    started = []
    partners = [at_z((mz + o) % Z) for o in range(1, Z)]
    partners += [at_q(q_of(o)) for o in range(1, Q)]
    partners += [at_t((ml + o) % YL, mc) for o in range(1, YL)]
    partners += [at_t(ml, 1 - mc)]
    barrier = pltpu.get_barrier_semaphore()
    for device in partners:
        pl.semaphore_signal(barrier, inc=1, device_id=device, device_id_type=MESH)

    w_copy = pltpu.make_async_copy(w_hbm, wv, w_sem.at[0])
    w_copy.start()
    wo_copy = pltpu.make_async_copy(wo_hbm, wo, w_sem.at[1])
    wo_copy.start()

    dst = dest[...]
    pack, slot = dst // TOK, dst % TOK
    iota_p = lax.broadcasted_iota(jnp.int32, (128, TOK), 0)
    of_pack = _onehot(iota_p == pack)
    before = _onehot(
        lax.broadcasted_iota(jnp.int32, (TOK, TOK), 0) < lax.broadcasted_iota(jnp.int32, (TOK, TOK), 1)
    )
    rank = jnp.sum(_nn(of_pack, before) * of_pack.astype(F32), axis=0, keepdims=True).astype(jnp.int32)
    px, pz, py = pack % X, (pack // X) % Z, pack // (X * Z)
    place = pz * s.B1 + (py * X + px) * s.CAP + rank
    pick = _onehot(lax.broadcasted_iota(jnp.int32, (Z * s.B1, TOK), 0) == place)
    slot1 = jnp.broadcast_to((slot + 1).astype(F32), (256 - W, TOK)).astype(BF16)
    s1[...] = _nt(pick, jnp.concatenate([ld[...], slot1], axis=0)).astype(BF16)

    pl.semaphore_wait(barrier, len(partners))

    zc = []
    for o in sorted(range(1, Z), key=lambda o: -min(o, Z - o)):
        to = (mz + o) % Z
        zc.append(
            send(rows(s1, to * s.B1, s.B1, 16), rows(r1, mz * s.B1, s.B1, 16),
                 z_ss.at[o - 1], z_rs.at[o - 1], at_z(to))
        )
    r1[pl.ds(pl.multiple_of(mz * s.B1, 16), s.B1)] = s1[pl.ds(pl.multiple_of(mz * s.B1, 16), s.B1)]

    def gather(src, buf, ss, rs, fs, fr):
        mine = rows(buf, tp * W, W, 16)
        first = [send(src, mine, fs.at[0], fr.at[0], at_t(ml, 1 - mc))]
        first += [send(src, mine, ss.at[o - 1], rs.at[o - 1], at_t((ml + o) % YL, mc)) for o in range(1, YL)]

        def rest():
            more = []
            for o in range(1, YL):
                first[o].wait_recv()
                there = rows(buf, ((ml - o + YL) % YL * C + mc) * W, W, 16)
                more.append(send(there, there, fs.at[o], fr.at[o], at_t(ml, 1 - mc)))
            first[0].wait_recv()
            for copy in more:
                copy.wait_recv()

        return rest

    cot_rest = gather(cot, ct, cg_ss, cg_rs, cf_ss, cf_rs)
    ct[pl.ds(pl.multiple_of(tp * W, 16), W)] = cot[...]

    w_copy.wait()
    for w in range(3):
        for j in range(0, s.D, 128):
            wn[w, pl.ds(j, 128)] = wv[pl.ds(w * W, W), pl.ds(j, 128)].T

    line = lax.broadcasted_iota(jnp.int32, (1, Z * s.B1), 1)
    inner = line % s.B1
    aim = inner // s.CAP * s.B2 + line // s.B1 * s.CAP + inner % s.CAP
    aim = jnp.where(inner < Q * s.CAP, aim, -1)
    regroup = _onehot(lax.broadcasted_iota(jnp.int32, (Q * s.B2, Z * s.B1), 0) == aim)
    for copy in zc:
        copy.wait_recv()
    s2[...] = _nn(regroup, r1[...]).astype(BF16)
    qc = []
    for o in range(1, Q):
        to = q_of(o)
        qc.append(
            send(rows(s2, to * s.B2, s.B2, 16), rows(r2, mq * s.B2, s.B2, 16),
                 q_ss.at[o - 1], q_rs.at[o - 1], at_q(to))
        )
    r2[pl.ds(pl.multiple_of(mq * s.B2, 16), s.B2)] = s2[pl.ds(pl.multiple_of(mq * s.B2, 16), s.B2)]

    cot_rest()
    wo_copy.wait()
    d_attn = _nn(wo[...], ct[...]).astype(BF16)

    for copy in qc:
        copy.wait_recv()
    got = r2[...]
    slots_got = got[:, W:W + 1].astype(F32)
    iota_s = lax.broadcasted_iota(jnp.int32, (Q * s.B2, TOK), 1).astype(F32) + 1.0
    put = _onehot(slots_got == iota_s)
    xt[pl.ds(pl.multiple_of(tp * W, 16), W)] = _tn(got, put)[:W].astype(BF16)
    rows_rest = gather(rows(xt, tp * W, W, 16), xt, xg_ss, xg_rs, xf_ss, xf_rs)
    rows_rest()

    qkv = _nn(wv[...], xt[...]).astype(BF16)
    scale = HEAD_DIM ** (-0.5)
    seg_to = jnp.broadcast_to(seg[...].astype(F32), (TOK, TOK))
    same = seg_to.T == seg_to
    heads = W // HEAD_DIM
    for h in range(heads):
        lo = h * HEAD_DIM
        qt = qkv[lo:lo + HEAD_DIM]
        kt = qkv[W + lo:W + lo + HEAD_DIM]
        vt = qkv[2 * W + lo:2 * W + lo + HEAD_DIM]
        da = d_attn[lo:lo + HEAD_DIM]
        scores = jnp.where(same, _tn(kt, qt) * scale, -jnp.inf)
        expo = jnp.exp(scores - jnp.max(scores, axis=0, keepdims=True))
        probs = expo / jnp.sum(expo, axis=0, keepdims=True)
        probs_b = probs.astype(BF16)
        attn = _nn(vt, probs_b).astype(BF16)
        d_prob = _tn(vt, da)
        delta = jnp.sum(da.astype(F32) * attn.astype(F32), axis=0, keepdims=True)
        d_score = (probs * (d_prob - delta) * scale).astype(BF16)
        dq3[0, lo:lo + HEAD_DIM] = _nn(kt, d_score).astype(BF16)
        dq3[1, lo:lo + HEAD_DIM] = _nt(qt, d_score).astype(BF16)
        dq3[2, lo:lo + HEAD_DIM] = _nt(da, probs_b).astype(BF16)
    dq3[:, W:] = jnp.zeros((3, 256 - W, TOK), BF16)

    f = (f0, f1)
    for t in range(s.T):
        block = xt[t * W:(t + 1) * W]
        for w in range(3):
            g = _nt(block, dq3[w])
            for h in range(2):
                f[h][pl.ds(t * 3 * W + w, W, stride=3)] = g[:, h * 128:(h + 1) * 128]

    def chunk(h, y, z, x, size):
        return f[h][pl.ds(pl.multiple_of(((y * Z + z) * X + x) * s.RPD, 8), size)]

    def rel(off):
        return (mz + off + Z) % Z

    steps = Z // 2

    a_len = YH * s.RZ // A_PARTS

    def a_own(p, off):
        per_y = A_PARTS // YH
        start = (p // per_y * Z + rel(off)) * s.RZ + p % per_y * a_len
        return f0[pl.ds(pl.multiple_of(start, 8), a_len)]

    a_copies = {}

    def a_step(k):
        for i in range(A_PARTS):
            for d in range(2):
                p = (i + d * A_PARTS // 2) % A_PARTS
                owner = p * 2 // A_PARTS
                if k == 1 and owner != d:
                    continue
                sign = 1 if d == 0 else -1
                term = a_own(p, sign * (steps + 1 - k))
                if k == (1 if owner == d else 2):
                    src = a_stage.at[p, d]
                else:
                    a_copies[d, p, k - 1].wait_recv()
                    src = a_slots.at[d, p, k - 2]
                    term = term + src[...].astype(F32)
                src[...] = term.astype(BF16)
                a_copies[d, p, k] = send(
                    src, a_slots.at[d, p, k - 1], a_ss.at[d, p, k - 1], a_rs.at[d, p, k - 1], at_z(rel(sign))
                )

    def a_total(p):
        value = a_own(p, 0)
        for d in range(2):
            a_copies[d, p, steps].wait_recv()
            value = value + a_slots[d, p, steps - 1].astype(F32)
        return value

    offs = [steps]
    cuts = [0, 1]
    for k in range(steps - 1, 0, -1):
        offs += [k, -k]
        cuts += [len(offs)]
    offs += [0]
    cuts += [len(offs)]
    two = 2 * s.RPD

    def of_x(h, off, x):
        return jnp.concatenate([chunk(h, y, rel(off), x, s.RPD) for y in range(YH)], axis=0)

    b_copies = {}

    def b_send(piece):
        lo, hi = cuts[piece], cuts[piece + 1]
        for o in range(1, X):
            to = (mx + o) % X
            for i in range(lo, hi):
                b_s[o - 1, i * two:(i + 1) * two] = of_x(1, offs[i], to).astype(BF16)
            span = pl.ds(lo * two, (hi - lo) * two)
            b_copies[piece, o] = send(b_s.at[o - 1, span], b_r.at[o - 1, span],
                                      b_ss.at[o - 1, piece], b_rs.at[o - 1, piece], at_q(my * X + to))

    def b_sum(piece):
        for o in range(1, X):
            b_copies[piece, o].wait_recv()
        for i in range(cuts[piece], cuts[piece + 1]):
            value = of_x(1, offs[i], mx)
            for o in range(1, X):
                value = value + b_r[o - 1, i * two:(i + 1) * two].astype(F32)
            b_f[i] = value

    half = -(-s.RPD // 16) * 16
    ends = (0, half, two)
    b_ring = {}

    def b_step(k):
        b_sum(k - 1)
        for d in range(2):
            sign = 1 if d == 0 else -1
            i = offs.index(sign * (steps + 1 - k)) if k > 1 else 0
            span = pl.ds(ends[d], ends[d + 1] - ends[d])
            if k == 1:
                b_stage[span] = b_f[i, span].astype(BF16)
                src, dst = b_stage.at[span], b_slots.at[d, 0, span]
            else:
                b_ring[d, k - 1].wait_recv()
                if k == 2:
                    b_f[i, span] = b_f[i, span] + b_slots[d, 0, span].astype(F32)
                    b_slots[d, 0] = b_f[i].astype(BF16)
                else:
                    b_slots[d, k - 2] = (b_f[i] + b_slots[d, k - 2].astype(F32)).astype(BF16)
                src, dst = b_slots.at[d, k - 2], b_slots.at[d, k - 1]
            b_ring[d, k] = send(src, dst, bz_ss.at[d, k - 1], bz_rs.at[d, k - 1], at_z(rel(sign)))

    def part(t):
        t = pl.multiple_of(t * W, 16)
        total = _nn(wn[0, pl.ds(t, W)], dq3[0, :W])
        total += _nn(wn[1, pl.ds(t, W)], dq3[1, :W])
        return total + _nn(wn[2, pl.ds(t, W)], dq3[2, :W])

    for piece in range(2):
        b_send(piece)
    a_step(1)
    for piece in range(2, len(cuts) - 1):
        b_send(piece)
    settle()
    for l in range(YL):
        ps_s[l] = part(l * C + 1 - mc).astype(BF16)
    pair = send(ps_s, ps_r, pc_ss, pc_rs, at_t(ml, 1 - mc))
    b_step(1)
    a_step(2)
    for l in range(YL):
        pown[l] = part(l * C + mc)
    pair.wait_recv()
    for l in range(YL):
        pown[l] = pown[l] + ps_r[l].astype(F32)
        py_s[l] = pown[l].astype(BF16)
    pc = []
    for o in range(1, YL):
        to = (ml + o) % YL
        pc.append(send(py_s.at[to], py_r.at[o - 1], py_ss.at[o - 1], py_rs.at[o - 1], at_t(to, mc)))
    for k in range(2, steps + 1):
        b_step(k)
        if k < steps:
            a_step(k + 1)
    b_sum(steps)
    value = b_f[len(offs) - 1]
    for d in range(2):
        b_ring[d, steps].wait_recv()
        value = value + b_slots[d, steps - 1].astype(F32)
    acc[...] = value
    other = 1 - my
    yc = send(acc.at[pl.ds(pl.multiple_of(other * s.RPD, 8), s.RPD)], yr, y_ss, y_rs, at_q(other * X + mx))

    for p in range(A_PARTS):
        red[p * a_len:(p + 1) * a_len] = a_total(p)

    def red_q(q):
        return red[pl.ds(pl.multiple_of(q * s.RPD, 8), s.RPD)]

    fill = jnp.zeros((xs.shape[1] - s.RPD, 128), F32)
    xc = []
    for o in range(1, Q):
        to = q_of(o)
        xs[o - 1] = jnp.concatenate([red_q(to), fill], axis=0).astype(BF16)
        xc.append(send(xs.at[o - 1], xr.at[o - 1], x_ss.at[o - 1], x_rs.at[o - 1], at_q(to)))
    settle()

    for copy in pc:
        copy.wait_recv()
    total = pown[ml]
    for o in range(1, YL):
        total = total + py_r[o - 1].astype(F32)
    d_out[...] = total.astype(BF16)

    value = red_q(mq)
    for o in range(1, Q):
        xc[o - 1].wait_recv()
        value = value + xr[o - 1, :s.RPD].astype(F32)
    yc.wait_recv()
    norm = (TOK * s.R) ** (-0.5)
    mine = pl.ds(pl.multiple_of(my * s.RPD, 8), s.RPD)
    g_out[:, :128] = value * norm
    g_out[:, 128:] = ((acc[mine] + yr[...]) * norm)[:, :W - 128]

    finish()


def shards(s, loader_rows, pack_dest, segment_ids, w_qkv, w_out, d_out):
    W, TOK, D = s.W, s.TOK, s.D
    Q, Z, X, YL = s.Q, s.Z, s.X, s.YL
    dma = pltpu.SemaphoreType.DMA
    vmem = pl.BlockSpec(memory_space=pltpu.VMEM)
    hbm = pl.BlockSpec(memory_space=pl.ANY)
    steps = Z // 2
    two = 2 * s.RPD
    grad, packed = pl.pallas_call(
        functools.partial(_kernel, s),
        out_shape=(
            jax.ShapeDtypeStruct((s.RPD, W), F32),
            jax.ShapeDtypeStruct((W, TOK), BF16),
        ),
        in_specs=[vmem, vmem, vmem, hbm, hbm, vmem],
        out_specs=(vmem, vmem),
        scratch_shapes=[
            pltpu.VMEM((3 * W, D), BF16),
            pltpu.VMEM((3, D, W), BF16),
            pltpu.VMEM((W, D), BF16),
            pltpu.VMEM((Z * s.B1, 256), BF16),
            pltpu.VMEM((Z * s.B1, 256), BF16),
            pltpu.VMEM((Q * s.B2, 256), BF16),
            pltpu.VMEM((Q * s.B2, 256), BF16),
            pltpu.VMEM((D, TOK), BF16),
            pltpu.VMEM((D, TOK), BF16),
            pltpu.VMEM((3, 256, TOK), BF16),
            pltpu.VMEM((3 * D, 128), F32),
            pltpu.VMEM((3 * D, 128), F32),
            pltpu.VMEM((A_PARTS, 2, 2 * s.RZ // A_PARTS, 128), BF16),
            pltpu.VMEM((2, A_PARTS, steps, 2 * s.RZ // A_PARTS, 128), BF16),
            pltpu.VMEM((X - 1, Z * two, 128), BF16),
            pltpu.VMEM((X - 1, Z * two, 128), BF16),
            pltpu.VMEM((Z, two, 128), F32),
            pltpu.VMEM((two, 128), BF16),
            pltpu.VMEM((2, steps, two, 128), BF16),
            pltpu.VMEM((2 * s.RZ, 128), F32),
            pltpu.VMEM((Q - 1, -(-s.RPD // 16) * 16, 128), BF16),
            pltpu.VMEM((Q - 1, -(-s.RPD // 16) * 16, 128), BF16),
            pltpu.VMEM((2 * s.RPD, 128), F32),
            pltpu.VMEM((s.RPD, 128), F32),
            pltpu.VMEM((YL, W, TOK), BF16),
            pltpu.VMEM((YL, W, TOK), BF16),
            pltpu.VMEM((YL, W, TOK), F32),
            pltpu.VMEM((YL, W, TOK), BF16),
            pltpu.VMEM((YL - 1, W, TOK), BF16),
            dma((2,)),
            dma((Z - 1,)),
            dma((Z - 1,)),
            dma((Q - 1,)),
            dma((Q - 1,)),
            dma((YL,)),
            dma((YL,)),
            dma((YL,)),
            dma((YL,)),
            dma((YL,)),
            dma((YL,)),
            dma((YL,)),
            dma((YL,)),
            dma((2, A_PARTS, steps)),
            dma((2, A_PARTS, steps)),
            dma((X - 1, steps + 1)),
            dma((X - 1, steps + 1)),
            dma((2, steps)),
            dma((2, steps)),
            dma((Q - 1,)),
            dma((Q - 1,)),
            dma,
            dma,
            dma,
            dma,
            dma((YL - 1,)),
            dma((YL - 1,)),
        ],
        compiler_params=pltpu.CompilerParams(
            collective_id=0, has_side_effects=True, vmem_limit_bytes=60 * 1024 * 1024
        ),
    )(
        loader_rows.T,
        pack_dest.reshape(1, TOK),
        segment_ids,
        jnp.transpose(w_qkv, (1, 2, 0)).reshape(3 * W, D),
        w_out,
        d_out.T,
    )
    return grad, packed.T


def build(mesh, s):
    placed = (
        P("rep", "tp"),
        P("rep"),
        P("rep", None),
        P(None, None, "tp"),
        P("tp", None),
        P("rep", "tp"),
    )
    return jax.shard_map(
        functools.partial(shards, s),
        mesh=mesh,
        in_specs=placed,
        out_specs=(P("rep", "tp"), P("rep", "tp")),
        check_vma=False,
    )


def solution(mesh):
    return build(mesh, Sizes(2, 12, 4, 4, 2, 256, 224))
```
